512 devices in a mesh: dp: 8 (over z_lo), block: 64 (over x, z_hi, y, core).
Axes of the slice: x: 4, y: 4, z: 16 (z_hi: 2, z_lo: 8; z = z_hi * 8 + z_lo), core: 2. Of those that a mesh axis runs over, the one named last changes fastest.
Arguments:
- features_in: bfloat16 [2048, 65536], P('dp', 'block'), may hold values from -6 to 6
- cotangent: bfloat16 [2048, 65536], P('dp', 'block'), may hold values from -6 to 6
- left_one: bfloat16 [256, 256, 256], P('block'), may hold values from -0.375 to 0.375
- right_one: bfloat16 [256, 256, 256], P('block'), may hold values from -0.375 to 0.375
- left_two: bfloat16 [256, 256, 256], P('block'), may hold values from -0.375 to 0.375
- right_two: bfloat16 [256, 256, 256], P('block'), may hold values from -0.375 to 0.375
Outputs:
- input_grad: bfloat16 [2048, 65536], P('dp', 'block')
- left_one_grad: float32 [256, 256, 256], P('dp', 'block')
- right_one_grad: float32 [256, 256, 256], P('dp', 'block')
- left_two_grad: float32 [256, 256, 256], P('dp', 'block')
- right_two_grad: float32 [256, 256, 256], P('dp', 'block')
The draws below stay inside these ranges and needn't reach their ends.
All inputs are finite; a program needn't handle non-finite values.
Results may differ from the reference program's by a relative error of at most 0.017.
Values may be sent and summed in bfloat16 or wider, within the bound.
A program may use at most 64 MiB of HBM per device.

```python
import jax
import jax.numpy as jnp

BLOCKS = 256
BLOCK_SIZE = 256
WIDTH = 65536
TOKENS = 2048


def level_of(own_key, shape, pieces, least, high):
    level = 1.0
    for dim, parts in pieces:
        steps = jax.random.uniform(jax.random.fold_in(jax.random.fold_in(own_key, 6), dim), (parts,), jnp.float32, least / len(pieces), high / len(pieces))
        level = level * jnp.repeat(jnp.exp(steps), shape[dim] // parts).reshape((-1,) + (1,) * (len(shape) - 1 - dim))
    return level


def gaussian(rng, shape, spread, bound, split=(), kind=jnp.bfloat16):
    loudness = level_of(rng, shape, split, -0.22, 0.18) if split else 1.0
    entries = jax.random.normal(rng, shape, jnp.float32) * spread * loudness
    return jnp.minimum(jnp.maximum(entries, -bound), bound).astype(kind)


def setup_inputs(seed: int = 0) -> dict:
    seeds = jax.random.split(jax.random.key(seed), 7)
    return {
        "features_in": gaussian(seeds[0], (TOKENS, WIDTH), 1.0, 6.0, ((0, 8), (1, 64))),
        "cotangent": gaussian(seeds[1], (TOKENS, WIDTH), 1.0, 6.0, ((0, 8), (1, 64))),
        "left_one": gaussian(seeds[2], (BLOCKS, BLOCK_SIZE, BLOCK_SIZE), BLOCK_SIZE ** -0.5, 0.375, ((0, 64),)),
        "right_one": gaussian(seeds[3], (BLOCKS, BLOCK_SIZE, BLOCK_SIZE), BLOCK_SIZE ** -0.5, 0.375, ((0, 64),)),
        "left_two": gaussian(seeds[4], (BLOCKS, BLOCK_SIZE, BLOCK_SIZE), BLOCK_SIZE ** -0.5, 0.375, ((0, 64),)),
        "right_two": gaussian(seeds[5], (BLOCKS, BLOCK_SIZE, BLOCK_SIZE), BLOCK_SIZE ** -0.5, 0.375, ((0, 64),)),
    }


def gelu_tanh(values):
    return jax.nn.gelu(values, approximate=True)

def swapped(values):
    return jnp.swapaxes(values, 1, 2)

def reference(features_in, cotangent, left_one, right_one, left_two, right_two):
    f32 = jnp.float32
    bf16 = jnp.bfloat16
    factor_scale = float(TOKENS) ** (-0.5)
    inputs3 = features_in.reshape(TOKENS, BLOCKS, BLOCK_SIZE).astype(f32)
    cot3 = cotangent.reshape(TOKENS, BLOCKS, BLOCK_SIZE).astype(f32)
    lone, rone = (left_one.astype(f32), right_one.astype(f32))
    ltwo, rtwo = (left_two.astype(f32), right_two.astype(f32))
    first_out = jnp.einsum('tji,jmi->tjm', inputs3, lone).astype(bf16)
    first_cols = swapped(first_out).astype(f32)
    hidden = swapped(jnp.einsum('tji,jmi->tjm', first_cols, rone)).astype(bf16)
    hidden32 = hidden.astype(f32)
    activated = gelu_tanh(hidden32).astype(bf16).astype(f32)
    second_out = jnp.einsum('tji,jmi->tjm', activated, ltwo).astype(bf16)
    second_cols = swapped(second_out).astype(f32)
    cot_cols = swapped(cot3)
    right_two_grad = jnp.einsum('tkm,tki->mki', cot_cols, second_cols) * factor_scale
    back_two = jnp.einsum('tkm,kmi->tki', cot_cols, rtwo).astype(bf16)
    back_rows = swapped(back_two).astype(f32)
    left_two_grad = jnp.einsum('tjm,tji->mji', back_rows, activated) * factor_scale
    grad_act = jnp.einsum('tjm,jmi->tji', back_rows, ltwo)
    _, pullback = jax.vjp(gelu_tanh, hidden32)
    grad_hidden = pullback(grad_act)[0].astype(bf16)
    hidden_cols = swapped(grad_hidden).astype(f32)
    right_one_grad = jnp.einsum('tkm,tki->mki', hidden_cols, first_cols) * factor_scale
    back_one = jnp.einsum('tkm,kmi->tki', hidden_cols, rone).astype(bf16)
    first_rows = swapped(back_one).astype(f32)
    left_one_grad = jnp.einsum('tjm,tji->mji', first_rows, inputs3) * factor_scale
    input_grad = jnp.einsum('tjm,jmi->tji', first_rows, lone).astype(bf16).reshape(TOKENS, WIDTH)
    return (input_grad, left_one_grad, right_one_grad, left_two_grad, right_two_grad)
```

```python
import jax
import jax.numpy as jnp
from jax import lax
from jax.experimental import pallas as pl
from jax.experimental.pallas import tpu as pltpu
from jax.sharding import PartitionSpec as P

MESH = pl.DeviceIdType.MESH
F32 = jnp.float32
BF16 = jnp.bfloat16
SIZE = 256
TOK = 128
PLANE = 32
NN = ((1,), (0,))
NT = ((1,), (1,))
TN = ((0,), (0,))


def dot(a, b, dims):
    return lax.dot_general(a, b, (dims, ((), ())), preferred_element_type=F32)


def selection(place):
    row = lax.broadcasted_iota(jnp.int32, (SIZE, SIZE), 0)
    col = lax.broadcasted_iota(jnp.int32, (SIZE, SIZE), 1)
    return (place(row) == col).astype(F32).astype(BF16)


def device_order(p):
    return (p & 192) + ((p >> 2) & 1) * 32 + ((p >> 3) & 7) * 4 + (p & 3)


def arrival_order(o):
    return ((o >> 2) & 3) * 64 + ((o >> 4) & 1) * 32 + (o & 3) * 8 + (o >> 5)


def gelu_parts(v):
    c = 0.7978845608028654
    th = jnp.tanh(c * (v + 0.044715 * (v * v * v)))
    return c, th


def gelu(v):
    _, th = gelu_parts(v)
    return 0.5 * v * (1.0 + th)


def gelu_slope(v):
    c, th = gelu_parts(v)
    return 0.5 * (1.0 + th) + 0.5 * v * (1.0 - th * th) * (c * (1.0 + 3.0 * 0.044715 * (v * v)))


def block_of(q, h):
    return (q // 8) * 16 + h * 8 + q % 8


def kernel(
    feat, cot, l1, r1, l2, r2,
    in_grad, g_l1, g_r1, g_l2, g_r2,
    perm, turn, eye,
    l1p, r1p, r1tp, l2p, l2t, r2tp, other,
    xs, xr, ps, pr,
    b1, dyk, hid, act, b2, da2, dwk, da1, back,
    part, part1, ring_s, ring_r, line_s, line_r,
    xs_sem, xr_sem, ps_sem, pr_sem, back_sem,
    gs_sem, gr_sem, rs_sem, rr_sem, ls_sem, lr_sem,
):
    zl = lax.axis_index("dp")
    blk = lax.axis_index("block")
    h = (blk // 8) % 2
    q = (blk // 16) * 8 + blk % 8
    z = h * 8 + zl
    scale = float(2048) ** (-0.5)

    def column(zz):
        return (zz % 8, block_of(q, zz // 8))

    up = column((z + 1) % 16)
    down = column((z + 15) % 16)
    across = (zl, block_of(q, 1 - h))

    barrier = pltpu.get_barrier_semaphore()

    def greet(i, carry):
        pl.semaphore_signal(barrier, inc=1, device_id=(zl, (blk + i) % 64), device_id_type=MESH)
        return carry

    lax.fori_loop(1, 64, greet, 0)
    pl.semaphore_signal(barrier, inc=1, device_id=up, device_id_type=MESH)
    pl.semaphore_signal(barrier, inc=1, device_id=down, device_id_type=MESH)
    pl.semaphore_wait(barrier, 65)

    factors = (r1, l2, r2)

    def gather_copy(way, k, src):
        return pltpu.make_async_remote_copy(
            src_ref=src,
            dst_ref=other.at[way, k],
            send_sem=gs_sem.at[way, k],
            recv_sem=gr_sem.at[way, k],
            device_id=up if way == 0 else down,
            device_id_type=MESH,
        )

    def gather_step(s):
        for way in range(2):
            place = zl if way == 0 else 7 - zl
            if s < 12:

                @pl.when(place == 7)
                def _():
                    own_half = factors[s // 4].at[2 * way + (s // 2) % 2, pl.ds((s % 2) * 128, 128)]
                    gather_copy(way, s, own_half).start()

            k = s - 1 - place

            @pl.when(jnp.logical_and(k >= 0, k < 12))
            def _():
                copy = gather_copy(way, k, other.at[way, k])
                copy.wait_recv()

                @pl.when(place < 7)
                def _():
                    copy.start()

    perm[...] = selection(device_order)
    turn[...] = selection(arrival_order)
    eye[...] = selection(lambda r: r)

    for jj in range(4):
        l1p[jj] = dot(perm[...], l1[jj], NN).astype(BF16)

    def cross_pack(n, left, rows):
        for pair in range(2):
            out = [
                dot(left(2 * pair + e), rows[:, pl.ds((2 * pair + e) * SIZE, SIZE)], NT)
                for e in range(2)
            ]
            for half in range(2):
                both = [o[:, half * TOK:(half + 1) * TOK].reshape(PLANE, 8, TOK) for o in out]
                xs[n, pl.ds(half * PLANE, PLANE), pl.ds(pair * 16, 16), :] = jnp.concatenate(
                    both, axis=1
                ).astype(BF16)

    def cross_launch(n, first, last):
        mine = q * 2 + h

        def send(i, carry):
            to = (blk + i) % 64
            to_h = (to // 8) % 2
            to_q = (to // 16) * 8 + to % 8
            pltpu.make_async_remote_copy(
                src_ref=xs.at[n, to_h * PLANE + to_q],
                dst_ref=xr.at[n, mine],
                send_sem=xs_sem.at[n],
                recv_sem=xr_sem.at[n],
                device_id=(zl, to),
                device_id_type=MESH,
            ).start()
            return carry

        lax.fori_loop(first, last, send, 0)
        if first == 1:
            pltpu.make_async_copy(xs.at[n, h * PLANE + q], xr.at[n, mine], xr_sem.at[n]).start()

    def take(group, g, out):
        rows = dot(turn[...], group, NN).astype(BF16).reshape(8, 2, 16, TOK)
        out[:, g // 2, :, g % 2] = rows

    def cross_take(n, out):
        pltpu.make_async_copy(xr.at[n], xr.at[n], xr_sem.at[n]).wait()

        def one(g, carry):
            take(xr[n, pl.ds(g * 8, 8)].reshape(SIZE, TOK), g, out)
            return carry

        lax.fori_loop(0, 8, one, 0)

    def plane_send(n, term):
        def one(pair, carry):
            both = [term(2 * pair + e).reshape(PLANE, 8, TOK) for e in range(2)]
            ps[n, :, pl.ds(pl.multiple_of(pair * 16, 16), 16), :] = jnp.concatenate(
                both, axis=1
            ).astype(BF16)
            return carry

        lax.fori_loop(0, 4, one, 0)

        def send(i, carry):
            to = (q + i) % PLANE
            pltpu.make_async_remote_copy(
                src_ref=ps.at[n, to],
                dst_ref=pr.at[n, q],
                send_sem=ps_sem.at[n],
                recv_sem=pr_sem.at[n],
                device_id=(zl, block_of(to, h)),
                device_id_type=MESH,
            ).start()
            return carry

        lax.fori_loop(1, PLANE, send, 0)
        pltpu.make_async_copy(ps.at[n, q], pr.at[n, q], pr_sem.at[n]).start()

    def plane_take(n, out):
        pltpu.make_async_copy(pr.at[n], pr.at[n], pr_sem.at[n]).wait()

        def one(g, carry):
            take(pr[n, pl.ds(g * 4, 4)].reshape(SIZE, TOK), g, out)
            return carry

        lax.fori_loop(0, 8, one, 0)

    def block(ref, k):
        return ref[k].reshape(SIZE, TOK)

    def own(n, d):
        return part[n, pl.ds((d // 8) * 4, 4), pl.ds(pl.multiple_of((d % 8) * 32, 32), 32), :]

    def ring_copy(n, way, s):
        return pltpu.make_async_remote_copy(
            src_ref=ring_s.at[n, way, s],
            dst_ref=ring_r.at[n, way, s],
            send_sem=rs_sem.at[n, way, s],
            recv_sem=rr_sem.at[n, way, s],
            device_id=up if way == 0 else down,
            device_id_type=MESH,
        )

    def ring_step(n, s):
        for way in range(2 if s < 7 else 1):
            d = (z + 8 - s) % 16 if way == 0 else (z + 9 + s) % 16
            total = own(n, d)
            if s:
                ring_copy(n, way, s - 1).wait_recv()
                total = total + ring_r[n, way, s - 1].astype(F32)
            ring_s[n, way, s] = total.astype(BF16)
            ring_copy(n, way, s).start()

    def ring_end(n, out):
        ring_copy(n, 0, 7).wait_recv()
        ring_copy(n, 1, 6).wait_recv()
        total = own(n, z) + ring_r[n, 0, 7].astype(F32) + ring_r[n, 1, 6].astype(F32)
        out[...] = total * scale

    def own_factor(f):
        return lambda b: factors[f][b]

    def other_factor(f):
        return lambda b: other[b // 2, pl.ds(f * 4 + (b % 2) * 2, 2)].reshape(SIZE, SIZE)

    def prepare(f, src, base):
        def one(b, carry):
            k = base + b
            m = src(b)
            if f == 0:
                r1p[k] = dot(perm[...], m, NN).astype(BF16)
                r1tp[k] = dot(perm[...], m, NT).astype(BF16)
            elif f == 1:
                l2p[k] = dot(perm[...], m, NN).astype(BF16)
                l2t[k] = dot(eye[...], m, NT).astype(BF16)
            else:
                r2tp[k] = dot(perm[...], m, NT).astype(BF16)
            return carry

        lax.fori_loop(0, 4, one, 0)

    def grad_hidden(k):
        grad = dot(l2t[k], block(da2, k), NN)
        grad = (grad * gelu_slope(block(hid, k).astype(F32))).astype(BF16)
        return dot(perm[...], grad, NN)

    def activate(k, carry):
        act[k] = gelu(hid[k].astype(F32)).astype(BF16)
        return carry

    def partial(n, left, right):
        def one(k, carry):
            part[n, k] = dot(block(left, k), block(right, k), NT)
            return carry

        lax.fori_loop(0, 8, one, 0)

    gather_step(0)
    cross_pack(0, lambda jj: l1p[jj], feat)
    cross_launch(0, 1, 64)
    gather_step(1)
    cross_pack(1, lambda jj: perm[...], cot)
    gather_step(2)
    for f in range(3):
        prepare(f, own_factor(f), h * 4)
    for s in range(3, 12):
        gather_step(s)
        cross_launch(1, 1 + 7 * (s - 3), 8 + 7 * (s - 3))
    prepare(0, other_factor(0), (1 - h) * 4)

    cross_take(0, b1)
    plane_send(0, lambda k: dot(r1p[k], block(b1, k), NN))
    for s in range(12, 16):
        gather_step(s)
    prepare(1, other_factor(1), (1 - h) * 4)
    plane_take(0, hid)
    lax.fori_loop(0, 8, activate, 0)
    plane_send(2, lambda k: dot(l2p[k], block(act, k), NN))
    for s in range(16, 20):
        gather_step(s)
    prepare(2, other_factor(2), (1 - h) * 4)
    plane_take(2, b2)

    cross_take(1, dyk)
    plane_send(1, lambda k: dot(r2tp[k], block(dyk, k), NN))
    partial(2, dyk, b2)
    ring_step(2, 0)
    plane_take(1, da2)
    plane_send(3, grad_hidden)
    ring_step(2, 1)
    partial(1, da2, act)
    ring_step(1, 0)
    plane_take(3, dwk)
    plane_send(4, lambda k: dot(r1tp[k], block(dwk, k), NN))
    ring_step(2, 2)
    ring_step(1, 1)
    partial(0, dwk, b1)
    ring_step(0, 0)
    plane_take(4, da1)
    back_copy = pltpu.make_async_remote_copy(
        src_ref=da1.at[pl.ds((1 - h) * 4, 4)],
        dst_ref=back,
        send_sem=back_sem.at[0],
        recv_sem=back_sem.at[1],
        device_id=across,
        device_id_type=MESH,
    )
    back_copy.start()
    for s in range(3, 8):
        ring_step(2, s)
        ring_step(1, s - 1)
        ring_step(0, s - 2)
    back_copy.wait_recv()

    def home_rows(which):
        return pl.ds(pl.multiple_of(which * TOK, TOK), TOK)

    for jj in range(4):
        mine = block(da1, h * 4 + jj)
        theirs = block(back, jj)
        cols = pl.ds(jj * SIZE, SIZE)
        part1[jj] = dot(mine, feat[home_rows(h), cols], NN) + dot(
            theirs, feat[home_rows(1 - h), cols], NN
        )

    def line_copy(way, s):
        return pltpu.make_async_remote_copy(
            src_ref=line_s.at[way, s],
            dst_ref=line_r.at[way, s],
            send_sem=ls_sem.at[way, s],
            recv_sem=lr_sem.at[way, s],
            device_id=up if way == 0 else down,
            device_id_type=MESH,
        )

    def own1(d):
        return part1[:, pl.ds(pl.multiple_of(d * 32, 32), 32), :]

    for s in range(7):
        for way in range(2):
            at = zl if way == 0 else 7 - zl
            d = 7 - (s - at) if way == 0 else s - at
            d = jnp.clip(d, 0, 7)

            @pl.when(jnp.logical_and(at <= s, at > 0))
            def _():
                if s:
                    line_copy(way, s - 1).wait_recv()
                    line_s[way, s] = (own1(d) + line_r[way, s - 1].astype(F32)).astype(BF16)
                    line_copy(way, s).start()

            @pl.when(at == 0)
            def _():
                line_s[way, s] = own1(d).astype(BF16)
                line_copy(way, s).start()

        if s == 0:
            for jj in range(4):
                cols = pl.ds(jj * SIZE, SIZE)
                in_grad[home_rows(h), cols] = dot(block(da1, h * 4 + jj), l1[jj], TN).astype(BF16)
                in_grad[home_rows(1 - h), cols] = dot(block(back, jj), l1[jj], TN).astype(BF16)
        if s == 1:
            ring_end(2, g_r2)
            ring_step(1, 7)
            ring_step(0, 6)
        if s == 3:
            ring_end(1, g_l2)
            ring_step(0, 7)
        if s == 5:
            ring_end(0, g_r1)

    g_l1[...] = own1(zl)
    for way in range(2):
        at = zl if way == 0 else 7 - zl

        @pl.when(at > 0)
        def _():
            line_copy(way, 6).wait_recv()
            g_l1[...] += line_r[way, 6].astype(F32)

    g_l1[...] = g_l1[...] * scale

    for n in range(2):
        sent = xs.at[n, pl.ds(0, 63)]
        pltpu.make_async_copy(sent, sent, xs_sem.at[n]).wait()
    for n in range(5):
        sent = ps.at[n, pl.ds(0, PLANE - 1)]
        pltpu.make_async_copy(sent, sent, ps_sem.at[n]).wait()
    back_copy.wait_send()
    for way in range(2):
        for k in range(12):
            gather_copy(way, k, other.at[way, k]).wait_send()
    for n in range(3):
        for s in range(8):
            ring_copy(n, 0, s).wait_send()
            if s < 7:
                ring_copy(n, 1, s).wait_send()
    for way in range(2):
        at = zl if way == 0 else 7 - zl
        for s in range(7):

            @pl.when(at <= s)
            def _():
                line_copy(way, s).wait_send()


def per_device(features_in, cotangent, left_one, right_one, left_two, right_two):
    vmem = pl.BlockSpec(memory_space=pltpu.VMEM)
    dma = pltpu.SemaphoreType.DMA
    square = (SIZE, SIZE)
    grad = jax.ShapeDtypeStruct((4, 32, SIZE), F32)
    arrived = pltpu.VMEM((8, 4, 2, 2, 16, TOK), BF16)
    eight = pltpu.VMEM((8,) + square, BF16)
    outs = pl.pallas_call(
        kernel,
        name="monarch",
        out_shape=(jax.ShapeDtypeStruct(features_in.shape, BF16), grad, grad, grad, grad),
        in_specs=[vmem] * 6,
        out_specs=(vmem,) * 5,
        scratch_shapes=[
            pltpu.VMEM(square, BF16),
            pltpu.VMEM(square, BF16),
            pltpu.VMEM(square, BF16),
            pltpu.VMEM((4,) + square, BF16),
            eight, eight, eight, eight, eight,
            pltpu.VMEM((2, 12, 128, SIZE), BF16),
            pltpu.VMEM((2, 64, 32, TOK), BF16),
            pltpu.VMEM((2, 64, 32, TOK), BF16),
            pltpu.VMEM((5, PLANE, 64, TOK), BF16),
            pltpu.VMEM((5, PLANE, 64, TOK), BF16),
            arrived, arrived, arrived, arrived, arrived, arrived, arrived, arrived,
            pltpu.VMEM((4, 4, 2, 2, 16, TOK), BF16),
            pltpu.VMEM((3, 8) + square, F32),
            pltpu.VMEM((4,) + square, F32),
            pltpu.VMEM((3, 2, 8, 4, 32, SIZE), BF16),
            pltpu.VMEM((3, 2, 8, 4, 32, SIZE), BF16),
            pltpu.VMEM((2, 7, 4, 32, SIZE), BF16),
            pltpu.VMEM((2, 7, 4, 32, SIZE), BF16),
            dma((2,)), dma((2,)), dma((5,)), dma((5,)), dma((2,)),
            dma((2, 12)), dma((2, 12)), dma((3, 2, 8)), dma((3, 2, 8)), dma((2, 7)), dma((2, 7)),
        ],
        compiler_params=pltpu.CompilerParams(
            collective_id=0, has_side_effects=True, vmem_limit_bytes=56 << 20
        ),
        cost_estimate=pl.CostEstimate(
            flops=4_000_000_000, bytes_accessed=5_000_000, transcendentals=600_000
        ),
    )(features_in, cotangent, left_one, right_one, left_two, right_two)
    return (outs[0],) + tuple(jnp.swapaxes(g, 0, 1) for g in outs[1:])


def solution(mesh):
    return jax.shard_map(
        per_device,
        mesh=mesh,
        in_specs=(
            P("dp", "block"),
            P("dp", "block"),
            P("block", None, None),
            P("block", None, None),
            P("block", None, None),
            P("block", None, None),
        ),
        out_specs=(
            P("dp", "block"),
            P("dp", "block", None),
            P("dp", "block", None),
            P("dp", "block", None),
            P("dp", "block", None),
        ),
        check_vma=False,
    )
```

```python
import jax
import jax.numpy as jnp
from jax import lax
from jax.experimental import pallas as pl
from jax.experimental.pallas import tpu as pltpu
from jax.sharding import PartitionSpec as P

MESH = pl.DeviceIdType.MESH
F32 = jnp.float32
BF16 = jnp.bfloat16
SIZE = 256
TOK = 128
PLANE = 32
NN = ((1,), (0,))
NT = ((1,), (1,))
TN = ((0,), (0,))


def dot(a, b, dims):
    return lax.dot_general(a, b, (dims, ((), ())), preferred_element_type=F32)


def selection(place):
    row = lax.broadcasted_iota(jnp.int32, (SIZE, SIZE), 0)
    col = lax.broadcasted_iota(jnp.int32, (SIZE, SIZE), 1)
    return (place(row) == col).astype(F32).astype(BF16)


def device_order(p):
    return (p & 192) + ((p >> 2) & 1) * 32 + ((p >> 3) & 7) * 4 + (p & 3)


def arrival_order(o):
    return ((o >> 2) & 3) * 64 + ((o >> 4) & 1) * 32 + (o & 3) * 8 + (o >> 5)


def gelu_parts(v):
    c = 0.7978845608028654
    th = jnp.tanh(c * (v + 0.044715 * (v * v * v)))
    return c, th


def gelu(v):
    _, th = gelu_parts(v)
    return 0.5 * v * (1.0 + th)


def gelu_slope(v):
    c, th = gelu_parts(v)
    return 0.5 * (1.0 + th) + 0.5 * v * (1.0 - th * th) * (c * (1.0 + 3.0 * 0.044715 * (v * v)))


def block_of(q, h):
    return ((q >> 3) << 4) + (h << 3) + (q & 7)


def kernel(
    feat, cot, l1, r1, l2, r2,
    in_grad, g_l1, g_r1, g_l2, g_r2,
    perm, turn, eye,
    l1p, r1p, r1tp, l2p, l2t, r2tp, other,
    xs, xr, ps, pr,
    b1, dyk, hid, act, b2, da2, dwk, da1, back,
    part, part1, last, ring_s, ring_r, line_s, line_r,
    xs_sem, xr_sem, ps_sem, pr_sem, back_sem,
    gs_sem, gr_sem, rs_sem, rr_sem, ls_sem, lr_sem,
):
    zl = lax.axis_index("dp")
    blk = lax.axis_index("block")
    h = (blk // 8) % 2
    q = (blk // 16) * 8 + blk % 8
    z = h * 8 + zl
    scale = float(2048) ** (-0.5)

    def column(zz):
        return (zz % 8, block_of(q, zz // 8))

    up = column((z + 1) % 16)
    down = column((z + 15) % 16)
    across = (zl, block_of(q, 1 - h))

    barrier = pltpu.get_barrier_semaphore()

    def greet(i, carry):
        pl.semaphore_signal(barrier, inc=1, device_id=(zl, (blk + i) & 63), device_id_type=MESH)
        return carry

    lax.fori_loop(1, 64, greet, 0)
    pl.semaphore_signal(barrier, inc=1, device_id=up, device_id_type=MESH)
    pl.semaphore_signal(barrier, inc=1, device_id=down, device_id_type=MESH)

    factors = (r1, l2, r2)

    def gather_copy(way, k, src):
        return pltpu.make_async_remote_copy(
            src_ref=src,
            dst_ref=other.at[way, k],
            send_sem=gs_sem.at[way, k],
            recv_sem=gr_sem.at[way, k],
            device_id=up if way == 0 else down,
            device_id_type=MESH,
        )

    def gather_source(f):
        for way in range(2):
            place = zl if way == 0 else 7 - zl

            @pl.when(place == 7)
            def _():
                for k in range(8):
                    own_half = factors[f].at[2 * way + k // 4, pl.ds((k % 4) * 64, 64)]
                    gather_copy(way, f * 8 + k, own_half).start()

    def gather_run(first, last, also=None):
        def one(when, carry):
            for way in range(2):
                place = zl if way == 0 else 7 - zl
                k = when - 3 * place

                @pl.when(jnp.logical_and(k >= 0, k < 24))
                def _():
                    copy = gather_copy(way, k, other.at[way, k])
                    copy.wait_recv()

                    @pl.when(place < 7)
                    def _():
                        copy.start()

            if also is not None:
                also(when)
            return carry

        lax.fori_loop(first, last, one, 0)

    perm[...] = selection(device_order)
    turn[...] = selection(arrival_order)
    eye[...] = selection(lambda r: r)

    for jj in range(4):
        l1p[jj] = dot(perm[...], l1[jj], NN).astype(BF16)

    def cross_pack(n, left, rows):
        for pair in range(2):
            out = [
                dot(left(2 * pair + e), rows[:, pl.ds((2 * pair + e) * SIZE, SIZE)], NT)
                for e in range(2)
            ]
            for half in range(2):
                both = [o[:, half * TOK:(half + 1) * TOK].reshape(PLANE, 8, TOK) for o in out]
                xs[n, pl.ds(half * PLANE, PLANE), pl.ds(pair * 16, 16), :] = jnp.concatenate(
                    both, axis=1
                ).astype(BF16)

    def cross_launch(n, first, last):
        mine = q * 2 + h

        def send(i, carry):
            to = (blk + i) & 63
            to_h = (to >> 3) & 1
            to_q = ((to >> 4) << 3) + (to & 7)
            pltpu.make_async_remote_copy(
                src_ref=xs.at[n, to_h * PLANE + to_q],
                dst_ref=xr.at[n, mine],
                send_sem=xs_sem.at[n],
                recv_sem=xr_sem.at[n],
                device_id=(zl, to),
                device_id_type=MESH,
            ).start()
            return carry

        lax.fori_loop(first, last, send, 0)

    def cross_own(n):
        pltpu.make_async_copy(
            xs.at[n, h * PLANE + q], xr.at[n, q * 2 + h], xr_sem.at[n]
        ).start()

    def take(groups, pair, out):
        rows = dot(turn[...], jnp.concatenate(groups, axis=1), NN).astype(BF16)
        for e in range(2):
            out[:, pair, :, e] = rows[:, e * TOK:(e + 1) * TOK].reshape(8, 2, 16, TOK)

    def cross_take(n, out):
        pltpu.make_async_copy(xr.at[n], xr.at[n], xr_sem.at[n]).wait()

        def one(pair, carry):
            groups = [xr[n, pl.ds(pair * 16 + e * 8, 8)].reshape(SIZE, TOK) for e in range(2)]
            take(groups, pair, out)
            return carry

        lax.fori_loop(0, 4, one, 0, unroll=True)

    def plane_send(n, term):
        def one(pair, carry):
            both = [term(2 * pair + e).reshape(PLANE, 8, TOK) for e in range(2)]
            ps[n, :, pl.ds(pl.multiple_of(pair * 16, 16), 16), :] = jnp.concatenate(
                both, axis=1
            ).astype(BF16)
            return carry

        lax.fori_loop(0, 4, one, 0, unroll=True)

        def send(i, carry):
            to = (q + i) & (PLANE - 1)
            pltpu.make_async_remote_copy(
                src_ref=ps.at[n, to],
                dst_ref=pr.at[n, q],
                send_sem=ps_sem.at[n],
                recv_sem=pr_sem.at[n],
                device_id=(zl, block_of(to, h)),
                device_id_type=MESH,
            ).start()
            return carry

        lax.fori_loop(1, PLANE, send, 0)
        pltpu.make_async_copy(ps.at[n, q], pr.at[n, q], pr_sem.at[n]).start()

    def plane_take(n, out):
        pltpu.make_async_copy(pr.at[n], pr.at[n], pr_sem.at[n]).wait()

        def one(pair, carry):
            groups = [pr[n, pl.ds(pair * 8 + e * 4, 4)].reshape(SIZE, TOK) for e in range(2)]
            take(groups, pair, out)
            return carry

        lax.fori_loop(0, 4, one, 0, unroll=True)

    def block(ref, k):
        return ref[k].reshape(SIZE, TOK)

    def own(n, d):
        return part[n, pl.ds((d // 8) * 4, 4), pl.ds(pl.multiple_of((d % 8) * 32, 32), 32), :]

    def ring_copy(n, way, s):
        return pltpu.make_async_remote_copy(
            src_ref=ring_s.at[n, way, s],
            dst_ref=ring_r.at[n, way, s],
            send_sem=rs_sem.at[n, way, s],
            recv_sem=rr_sem.at[n, way, s],
            device_id=up if way == 0 else down,
            device_id_type=MESH,
        )

    def ring_step(n, s):
        for way in range(2 if s < 7 else 1):
            d = (z + 8 - s) % 16 if way == 0 else (z + 9 + s) % 16
            total = own(n, d)
            if s:
                ring_copy(n, way, s - 1).wait_recv()
                total = total + ring_r[n, way, s - 1].astype(F32)
            ring_s[n, way, s] = total.astype(BF16)
            ring_copy(n, way, s).start()

    def ring_end(n, out):
        ring_copy(n, 0, 7).wait_recv()
        ring_copy(n, 1, 6).wait_recv()
        total = own(n, z) + ring_r[n, 0, 7].astype(F32) + ring_r[n, 1, 6].astype(F32)
        for j in range(4):
            out[:, j, :] = total[j] * scale

    def own_factor(f):
        return lambda b: factors[f][b]

    def other_factor(f):
        return lambda b: other[b // 2, pl.ds(f * 8 + (b % 2) * 4, 4)].reshape(SIZE, SIZE)

    def prepare(f, src, base):
        def one(b, carry):
            k = base + b
            m = src(b)
            if f == 0:
                r1p[k] = dot(perm[...], m, NN).astype(BF16)
                r1tp[k] = dot(perm[...], m, NT).astype(BF16)
            elif f == 1:
                l2p[k] = dot(perm[...], m, NN).astype(BF16)
                l2t[k] = dot(eye[...], m, NT).astype(BF16)
            else:
                r2tp[k] = dot(perm[...], m, NT).astype(BF16)
            return carry

        lax.fori_loop(0, 4, one, 0, unroll=True)

    def grad_hidden(k):
        grad = dot(l2t[k], block(da2, k), NN)
        grad = (grad * gelu_slope(block(hid, k).astype(F32))).astype(BF16)
        return dot(perm[...], grad, NN)

    def activate(k, carry):
        act[k] = gelu(hid[k].astype(F32)).astype(BF16)
        return carry

    def partial(n, left, right):
        def one(k, carry):
            part[n, k] = dot(block(left, k), block(right, k), NT)
            return carry

        lax.fori_loop(0, 8, one, 0, unroll=True)

    cross_pack(0, lambda jj: l1p[jj], feat)
    pl.semaphore_wait(barrier, 65)
    gather_source(0)
    cross_own(0)
    gather_source(1)
    cross_pack(1, lambda jj: perm[...], cot)
    cross_own(1)
    gather_source(2)
    for f in range(3):
        prepare(f, own_factor(f), h * 4)
    def pace(when):
        cross_launch(0, jnp.minimum(3 * when + 1, 64), jnp.minimum(3 * when + 4, 64))
        late = jnp.maximum(when - 22, 0)
        cross_launch(
            1, jnp.minimum(3 * late + 1, 64),
            jnp.where(when < 22, 1, jnp.minimum(3 * late + 4, 64)),
        )

    gather_run(0, 29, pace)
    prepare(0, other_factor(0), (1 - h) * 4)

    cross_take(0, b1)
    plane_send(0, lambda k: dot(r1p[k], block(b1, k), NN))
    gather_run(29, 37, pace)
    prepare(1, other_factor(1), (1 - h) * 4)
    plane_take(0, hid)
    lax.fori_loop(0, 8, activate, 0, unroll=True)
    plane_send(2, lambda k: dot(l2p[k], block(act, k), NN))
    gather_run(37, 45, pace)
    prepare(2, other_factor(2), (1 - h) * 4)
    plane_take(2, b2)

    cross_take(1, dyk)
    plane_send(1, lambda k: dot(r2tp[k], block(dyk, k), NN))
    partial(2, dyk, b2)
    ring_step(2, 0)
    ring_step(2, 1)
    plane_take(1, da2)
    plane_send(3, grad_hidden)
    ring_step(2, 2)
    partial(1, da2, act)
    ring_step(1, 0)
    ring_step(2, 3)
    ring_step(1, 1)
    plane_take(3, dwk)
    plane_send(4, lambda k: dot(r1tp[k], block(dwk, k), NN))
    ring_step(2, 4)
    ring_step(1, 2)
    partial(0, dwk, b1)
    ring_step(0, 0)
    ring_step(2, 5)
    ring_step(1, 3)
    ring_step(0, 1)
    plane_take(4, da1)
    def back_copy(c):
        return pltpu.make_async_remote_copy(
            src_ref=da1.at[pl.ds((1 - h) * 4, 4), c // 2, c % 2],
            dst_ref=back.at[pl.ds(0, 4), c // 2, c % 2],
            send_sem=back_sem.at[0, c],
            recv_sem=back_sem.at[1, c],
            device_id=across,
            device_id_type=MESH,
        )

    for c in (7, 0, 6, 1, 5, 2, 4, 3):
        back_copy(c).start()

    def home_rows(which):
        return pl.ds(pl.multiple_of(which * TOK, TOK), TOK)

    for jj in range(4):
        mine = block(da1, h * 4 + jj)
        part1[jj] = dot(mine, feat[home_rows(h), pl.ds(jj * SIZE, SIZE)], NN)

    def home_part(c):
        back_copy(c).wait_recv()
        for jj in range(4):
            theirs = back[jj, c // 2, c % 2].reshape(32, TOK)
            part1[jj, pl.ds(c * 32, 32)] += dot(
                theirs, feat[home_rows(1 - h), pl.ds(jj * SIZE, SIZE)], NN
            )

    def ring_steps(*steps):
        for n, s in steps:
            ring_step(n, s)

    ring_steps((2, 6), (1, 4), (0, 2))

    def line_copy(way, s):
        return pltpu.make_async_remote_copy(
            src_ref=line_s.at[way, s],
            dst_ref=line_r.at[way, s],
            send_sem=ls_sem.at[way, s],
            recv_sem=lr_sem.at[way, s],
            device_id=up if way == 0 else down,
            device_id_type=MESH,
        )

    def own1(d):
        return part1[:, pl.ds(pl.multiple_of(d * 32, 32), 32), :]

    for s in range(7):
        if s < 4:
            home_part(7 - s)
            home_part(s)
        for way in range(2):
            at = zl if way == 0 else 7 - zl
            d = 7 - (s - at) if way == 0 else s - at
            d = jnp.clip(d, 0, 7)

            @pl.when(jnp.logical_and(at <= s, at > 0))
            def _():
                if s:
                    line_copy(way, s - 1).wait_recv()
                    line_s[way, s] = (own1(d) + line_r[way, s - 1].astype(F32)).astype(BF16)
                    line_copy(way, s).start()

            @pl.when(at == 0)
            def _():
                line_s[way, s] = own1(d).astype(BF16)
                line_copy(way, s).start()

        if s == 0:
            ring_steps((2, 7), (1, 5), (0, 3))
        if s == 1:
            ring_end(2, g_r2)
            ring_steps((1, 6), (0, 4))
        if s == 2:
            ring_steps((1, 7), (0, 5))
        if s == 3:
            ring_end(1, g_l2)
            ring_step(0, 6)
        if s == 4:
            for jj in range(4):
                cols = pl.ds(jj * SIZE, SIZE)
                in_grad[home_rows(h), cols] = dot(block(da1, h * 4 + jj), l1[jj], TN).astype(BF16)
                in_grad[home_rows(1 - h), cols] = dot(block(back, jj), l1[jj], TN).astype(BF16)
            ring_step(0, 7)
        if s == 6:
            ring_end(0, g_r1)

    last[...] = own1(zl)
    for way in range(2):
        at = zl if way == 0 else 7 - zl

        @pl.when(at > 0)
        def _():
            line_copy(way, 6).wait_recv()
            last[...] += line_r[way, 6].astype(F32)

    for j in range(4):
        g_l1[:, j, :] = last[j] * scale

    for n in range(2):
        sent = xs.at[n, pl.ds(0, 63)]
        pltpu.make_async_copy(sent, sent, xs_sem.at[n]).wait()
    for n in range(5):
        sent = ps.at[n, pl.ds(0, PLANE - 1)]
        pltpu.make_async_copy(sent, sent, ps_sem.at[n]).wait()
    for c in range(8):
        back_copy(c).wait_send()
    for way in range(2):
        for k in range(24):
            gather_copy(way, k, other.at[way, k]).wait_send()
    for n in range(3):
        for s in range(8):
            ring_copy(n, 0, s).wait_send()
            if s < 7:
                ring_copy(n, 1, s).wait_send()
    for way in range(2):
        at = zl if way == 0 else 7 - zl
        for s in range(7):

            @pl.when(at <= s)
            def _():
                line_copy(way, s).wait_send()


def per_device(features_in, cotangent, left_one, right_one, left_two, right_two):
    vmem = pl.BlockSpec(memory_space=pltpu.VMEM)
    dma = pltpu.SemaphoreType.DMA
    square = (SIZE, SIZE)
    grad = jax.ShapeDtypeStruct((32, 4, SIZE), F32)
    arrived = pltpu.VMEM((8, 4, 2, 2, 16, TOK), BF16)
    eight = pltpu.VMEM((8,) + square, BF16)
    outs = pl.pallas_call(
        kernel,
        name="monarch",
        out_shape=(jax.ShapeDtypeStruct(features_in.shape, BF16), grad, grad, grad, grad),
        in_specs=[vmem] * 6,
        out_specs=(vmem,) * 5,
        scratch_shapes=[
            pltpu.VMEM(square, BF16),
            pltpu.VMEM(square, BF16),
            pltpu.VMEM(square, BF16),
            pltpu.VMEM((4,) + square, BF16),
            eight, eight, eight, eight, eight,
            pltpu.VMEM((2, 24, 64, SIZE), BF16),
            pltpu.VMEM((2, 64, 32, TOK), BF16),
            pltpu.VMEM((2, 64, 32, TOK), BF16),
            pltpu.VMEM((5, PLANE, 64, TOK), BF16),
            pltpu.VMEM((5, PLANE, 64, TOK), BF16),
            arrived, arrived, arrived, arrived, arrived, arrived, arrived, arrived,
            pltpu.VMEM((4, 4, 2, 2, 16, TOK), BF16),
            pltpu.VMEM((3, 8) + square, F32),
            pltpu.VMEM((4,) + square, F32),
            pltpu.VMEM((4, 32, SIZE), F32),
            pltpu.VMEM((3, 2, 8, 4, 32, SIZE), BF16),
            pltpu.VMEM((3, 2, 8, 4, 32, SIZE), BF16),
            pltpu.VMEM((2, 7, 4, 32, SIZE), BF16),
            pltpu.VMEM((2, 7, 4, 32, SIZE), BF16),
            dma((2,)), dma((2,)), dma((5,)), dma((5,)), dma((2, 8)),
            dma((2, 24)), dma((2, 24)), dma((3, 2, 8)), dma((3, 2, 8)), dma((2, 7)), dma((2, 7)),
        ],
        compiler_params=pltpu.CompilerParams(
            collective_id=0, has_side_effects=True, vmem_limit_bytes=56 << 20
        ),
        cost_estimate=pl.CostEstimate(
            flops=4_000_000_000, bytes_accessed=5_000_000, transcendentals=600_000
        ),
    )(features_in, cotangent, left_one, right_one, left_two, right_two)
    return outs


def solution(mesh):
    return jax.shard_map(
        per_device,
        mesh=mesh,
        in_specs=(
            P("dp", "block"),
            P("dp", "block"),
            P("block", None, None),
            P("block", None, None),
            P("block", None, None),
            P("block", None, None),
        ),
        out_specs=(
            P("dp", "block"),
            P("dp", "block", None),
            P("dp", "block", None),
            P("dp", "block", None),
            P("dp", "block", None),
        ),
        check_vma=False,
    )
```

```python
import jax
import jax.numpy as jnp
from jax import lax
from jax.experimental import pallas as pl
from jax.experimental.pallas import tpu as pltpu
from jax.sharding import PartitionSpec as P

MESH = pl.DeviceIdType.MESH
F32 = jnp.float32
BF16 = jnp.bfloat16
SIZE = 256
TOK = 128
PLANE = 32
PARTNERS = sorted(
    ((dx, dy, dc) for dx in range(4) for dy in range(4) for dc in range(2) if (dx, dy, dc) != (0, 0, 0)),
    key=lambda o: -(min(o[0], 4 - o[0]) + min(o[1], 4 - o[1])),
)
NN = ((1,), (0,))
NT = ((1,), (1,))
TN = ((0,), (0,))


def dot(a, b, dims):
    return lax.dot_general(a, b, (dims, ((), ())), preferred_element_type=F32)


def selection(place):
    row = lax.broadcasted_iota(jnp.int32, (SIZE, SIZE), 0)
    col = lax.broadcasted_iota(jnp.int32, (SIZE, SIZE), 1)
    return (place(row) == col).astype(F32).astype(BF16)


def device_order(p):
    return (p & 192) + ((p >> 2) & 1) * 32 + ((p >> 3) & 7) * 4 + (p & 3)


def arrival_order(o):
    return ((o >> 2) & 3) * 64 + ((o >> 4) & 1) * 32 + (o & 3) * 8 + (o >> 5)


def gelu_parts(v):
    c = 0.7978845608028654
    th = jnp.tanh(c * (v + 0.044715 * (v * v * v)))
    return c, th


def gelu(v):
    _, th = gelu_parts(v)
    return 0.5 * v * (1.0 + th)


def gelu_slope(v):
    c, th = gelu_parts(v)
    return 0.5 * (1.0 + th) + 0.5 * v * (1.0 - th * th) * (c * (1.0 + 3.0 * 0.044715 * (v * v)))


def block_of(q, h):
    return ((q >> 3) << 4) + (h << 3) + (q & 7)


def kernel(
    feat_in, cot_in, l1_in, r1_in, l2_in, r2_in,
    in_grad, g_l1, g_r1, g_l2, g_r2,
    feat, cot, l1, r1, l2, r2, load_sem,
    perm, turn, eye,
    l1p, r1p, r1tp, l2p, l2t, r2tp, other,
    xs, xr, ps, pr,
    b1, dyk, hid, slope, act, b2, da2, dwk, da1, back,
    part, part1, last, ring_s, ring_r, line_s, line_r,
    xs_sem, xr_sem, ps_sem, pr_sem, back_sem,
    gs_sem, gr_sem, rs_sem, rr_sem, ls_sem, lr_sem,
):
    zl = lax.axis_index("dp")
    blk = lax.axis_index("block")
    h = (blk // 8) % 2
    q = (blk // 16) * 8 + blk % 8
    z = h * 8 + zl
    scale = float(2048) ** (-0.5)

    def column(zz):
        return (zz % 8, block_of(q, zz // 8))

    up = column((z + 1) % 16)
    down = column((z + 15) % 16)
    across = (zl, block_of(q, 1 - h))

    loads = [
        pltpu.make_async_copy(src, dst, load_sem.at[i])
        for i, (src, dst) in enumerate(
            ((feat_in, feat), (l1_in, l1), (r1_in, r1), (cot_in, cot), (l2_in, l2), (r2_in, r2))
        )
    ]
    for load in loads:
        load.start()

    barrier = pltpu.get_barrier_semaphore()

    def greet(i, carry):
        pl.semaphore_signal(barrier, inc=1, device_id=(zl, (blk + i) & 63), device_id_type=MESH)
        return carry

    lax.fori_loop(1, 64, greet, 0)
    pl.semaphore_signal(barrier, inc=1, device_id=up, device_id_type=MESH)
    pl.semaphore_signal(barrier, inc=1, device_id=down, device_id_type=MESH)

    factors = (r1, l2, r2)

    def gather_copy(way, k, src):
        return pltpu.make_async_remote_copy(
            src_ref=src,
            dst_ref=other.at[way, k],
            send_sem=gs_sem.at[way, k],
            recv_sem=gr_sem.at[way, k],
            device_id=up if way == 0 else down,
            device_id_type=MESH,
        )

    def gather_source(f):
        for way in range(2):
            place = zl if way == 0 else 7 - zl

            @pl.when(place == 7)
            def _():
                for k in range(8):
                    own_half = factors[f].at[2 * way + k // 4, pl.ds((k % 4) * 64, 64)]
                    gather_copy(way, f * 8 + k, own_half).start()

    def gather_run(first, last, also=None):
        def one(when, carry):
            for way in range(2):
                place = zl if way == 0 else 7 - zl
                k = when - 3 * place

                @pl.when(jnp.logical_and(k >= 0, k < 24))
                def _():
                    copy = gather_copy(way, k, other.at[way, k])
                    copy.wait_recv()

                    @pl.when(place < 7)
                    def _():
                        copy.start()

            if also is not None:
                also(when)
            return carry

        lax.fori_loop(first, last, one, 0)

    perm[...] = selection(device_order)
    turn[...] = selection(arrival_order)
    eye[...] = selection(lambda r: r)

    loads[0].wait()
    loads[1].wait()
    for jj in range(4):
        l1p[jj] = dot(perm[...], l1[jj], NN).astype(BF16)

    def cross_pack(n, left, rows):
        for pair in range(2):
            out = [
                dot(left(2 * pair + e), rows[:, pl.ds((2 * pair + e) * SIZE, SIZE)], NT)
                for e in range(2)
            ]
            for half in range(2):
                both = [o[:, half * TOK:(half + 1) * TOK].reshape(PLANE, 8, TOK) for o in out]
                xs[n, pl.ds(half * PLANE, PLANE), pl.ds(pair * 16, 16), :] = jnp.concatenate(
                    both, axis=1
                ).astype(BF16)

    def cross_launch(n, first, last):
        mine = q * 2 + h

        def send(i, carry):
            to = (blk + i) & 63
            to_h = (to >> 3) & 1
            to_q = ((to >> 4) << 3) + (to & 7)
            pltpu.make_async_remote_copy(
                src_ref=xs.at[n, to_h * PLANE + to_q],
                dst_ref=xr.at[n, mine],
                send_sem=xs_sem.at[n],
                recv_sem=xr_sem.at[n],
                device_id=(zl, to),
                device_id_type=MESH,
            ).start()
            return carry

        lax.fori_loop(first, last, send, 0)

    def cross_own(n):
        pltpu.make_async_copy(
            xs.at[n, h * PLANE + q], xr.at[n, q * 2 + h], xr_sem.at[n]
        ).start()

    def take(groups, pair, out):
        rows = dot(turn[...], jnp.concatenate(groups, axis=1), NN).astype(BF16)
        for e in range(2):
            out[:, pair, :, e] = rows[:, e * TOK:(e + 1) * TOK].reshape(8, 2, 16, TOK)

    def cross_take(n, out):
        pltpu.make_async_copy(xr.at[n], xr.at[n], xr_sem.at[n]).wait()

        def one(pair, carry):
            groups = [xr[n, pl.ds(pair * 16 + e * 8, 8)].reshape(SIZE, TOK) for e in range(2)]
            take(groups, pair, out)
            return carry

        lax.fori_loop(0, 4, one, 0, unroll=True)

    def plane_send(n, term):
        def one(pair, carry):
            both = [term(2 * pair + e).reshape(PLANE, 8, TOK) for e in range(2)]
            ps[n, :, pl.ds(pl.multiple_of(pair * 16, 16), 16), :] = jnp.concatenate(
                both, axis=1
            ).astype(BF16)
            return carry

        lax.fori_loop(0, 4, one, 0, unroll=True)

        for dx, dy, dc in PARTNERS:
            to = (((q >> 3) + dx) & 3) * 8 + (((q >> 1) + dy) & 3) * 2 + ((q + dc) & 1)
            pltpu.make_async_remote_copy(
                src_ref=ps.at[n, to],
                dst_ref=pr.at[n, q],
                send_sem=ps_sem.at[n],
                recv_sem=pr_sem.at[n],
                device_id=(zl, block_of(to, h)),
                device_id_type=MESH,
            ).start()
        pltpu.make_async_copy(ps.at[n, q], pr.at[n, q], pr_sem.at[n]).start()

    def plane_take(n, out):
        pltpu.make_async_copy(pr.at[n], pr.at[n], pr_sem.at[n]).wait()

        def one(pair, carry):
            groups = [pr[n, pl.ds(pair * 8 + e * 4, 4)].reshape(SIZE, TOK) for e in range(2)]
            take(groups, pair, out)
            return carry

        lax.fori_loop(0, 4, one, 0, unroll=True)

    def block(ref, k):
        return ref[k].reshape(SIZE, TOK)

    def own(n, d):
        return part[n, pl.ds((d // 8) * 4, 4), pl.ds(pl.multiple_of((d % 8) * 32, 32), 32), :]

    def ring_copy(n, way, s):
        return pltpu.make_async_remote_copy(
            src_ref=ring_s.at[n, way, s],
            dst_ref=ring_r.at[n, way, s],
            send_sem=rs_sem.at[n, way, s],
            recv_sem=rr_sem.at[n, way, s],
            device_id=up if way == 0 else down,
            device_id_type=MESH,
        )

    def ring_step(n, s):
        for way in range(2 if s < 7 else 1):
            d = (z + 8 - s) % 16 if way == 0 else (z + 9 + s) % 16
            total = own(n, d)
            if s:
                ring_copy(n, way, s - 1).wait_recv()
                total = total + ring_r[n, way, s - 1].astype(F32)
            ring_s[n, way, s] = total.astype(BF16)
            ring_copy(n, way, s).start()

    def ring_end(n, out):
        ring_copy(n, 0, 7).wait_recv()
        ring_copy(n, 1, 6).wait_recv()
        total = own(n, z) + ring_r[n, 0, 7].astype(F32) + ring_r[n, 1, 6].astype(F32)
        for j in range(4):
            out[:, j, :] = total[j] * scale

    def own_factor(f):
        return lambda b: factors[f][b]

    def other_factor(f):
        return lambda b: other[b // 2, pl.ds(f * 8 + (b % 2) * 4, 4)].reshape(SIZE, SIZE)

    def prepare(f, src, base):
        def one(b, carry):
            k = base + b
            m = src(b)
            if f == 0:
                r1p[k] = dot(perm[...], m, NN).astype(BF16)
                r1tp[k] = dot(perm[...], m, NT).astype(BF16)
            elif f == 1:
                l2p[k] = dot(perm[...], m, NN).astype(BF16)
                l2t[k] = dot(eye[...], m, NT).astype(BF16)
            else:
                r2tp[k] = dot(perm[...], m, NT).astype(BF16)
            return carry

        lax.fori_loop(0, 4, one, 0, unroll=True)

    def grad_hidden(k):
        grad = dot(l2t[k], block(da2, k), NN)
        grad = (grad * block(slope, k)).astype(BF16)
        return dot(perm[...], grad, NN)

    def activate(k, carry):
        act[k] = gelu(hid[k].astype(F32)).astype(BF16)
        return carry

    def derive(k, carry):
        slope[k] = gelu_slope(hid[k].astype(F32))
        return carry

    def partial(n, left, right):
        def one(k, carry):
            part[n, k] = dot(block(left, k), block(right, k), NT)
            return carry

        lax.fori_loop(0, 8, one, 0, unroll=True)

    cross_pack(0, lambda jj: l1p[jj], feat)
    for load in loads[2:]:
        load.wait()
    pl.semaphore_wait(barrier, 65)
    gather_source(0)
    cross_own(0)
    gather_source(1)
    cross_pack(1, lambda jj: perm[...], cot)
    cross_own(1)
    gather_source(2)
    for f in range(3):
        prepare(f, own_factor(f), h * 4)
    def pace(when):
        cross_launch(0, jnp.minimum(3 * when + 1, 64), jnp.minimum(3 * when + 4, 64))
        late = jnp.maximum(when - 22, 0)
        cross_launch(
            1, jnp.minimum(3 * late + 1, 64),
            jnp.where(when < 22, 1, jnp.minimum(3 * late + 4, 64)),
        )

    gather_run(0, 29, pace)
    prepare(0, other_factor(0), (1 - h) * 4)

    cross_take(0, b1)
    plane_send(0, lambda k: dot(r1p[k], block(b1, k), NN))
    gather_run(29, 37, pace)
    prepare(1, other_factor(1), (1 - h) * 4)
    plane_take(0, hid)
    lax.fori_loop(0, 8, activate, 0, unroll=True)
    plane_send(2, lambda k: dot(l2p[k], block(act, k), NN))
    gather_run(37, 45, pace)
    prepare(2, other_factor(2), (1 - h) * 4)
    plane_take(2, b2)
    lax.fori_loop(0, 8, derive, 0, unroll=True)

    cross_take(1, dyk)
    plane_send(1, lambda k: dot(r2tp[k], block(dyk, k), NN))
    partial(2, dyk, b2)
    ring_step(2, 0)
    ring_step(2, 1)
    plane_take(1, da2)
    plane_send(3, grad_hidden)
    ring_step(2, 2)
    partial(1, da2, act)
    ring_step(1, 0)
    ring_step(2, 3)
    ring_step(1, 1)
    plane_take(3, dwk)
    plane_send(4, lambda k: dot(r1tp[k], block(dwk, k), NN))
    ring_step(2, 4)
    ring_step(1, 2)
    partial(0, dwk, b1)
    ring_step(0, 0)
    ring_step(2, 5)
    ring_step(1, 3)
    ring_step(0, 1)
    plane_take(4, da1)
    def back_copy(c):
        return pltpu.make_async_remote_copy(
            src_ref=da1.at[pl.ds((1 - h) * 4, 4), c // 2, c % 2],
            dst_ref=back.at[pl.ds(0, 4), c // 2, c % 2],
            send_sem=back_sem.at[0, c],
            recv_sem=back_sem.at[1, c],
            device_id=across,
            device_id_type=MESH,
        )

    for c in (7, 0, 6, 1, 5, 2, 4, 3):
        back_copy(c).start()

    def home_rows(which):
        return pl.ds(pl.multiple_of(which * TOK, TOK), TOK)

    for jj in range(4):
        mine = block(da1, h * 4 + jj)
        part1[jj] = dot(mine, feat[home_rows(h), pl.ds(jj * SIZE, SIZE)], NN)

    def home_part(c):
        back_copy(c).wait_recv()
        for jj in range(4):
            theirs = back[jj, c // 2, c % 2].reshape(32, TOK)
            part1[jj, pl.ds(c * 32, 32)] += dot(
                theirs, feat[home_rows(1 - h), pl.ds(jj * SIZE, SIZE)], NN
            )

    def ring_steps(*steps):
        for n, s in steps:
            ring_step(n, s)

    ring_steps((2, 6), (1, 4), (0, 2))

    def line_copy(way, s, e):
        return pltpu.make_async_remote_copy(
            src_ref=line_s.at[way, s, e],
            dst_ref=line_r.at[way, s, e],
            send_sem=ls_sem.at[way, s, e],
            recv_sem=lr_sem.at[way, s, e],
            device_id=up if way == 0 else down,
            device_id_type=MESH,
        )

    def own1(d, e):
        return part1[pl.ds(2 * e, 2), pl.ds(pl.multiple_of(d * 32, 32), 32), :]

    for s in range(7):
        if s < 4:
            home_part(7 - s)
            home_part(s)
        for e in range(2):
            for way in range(2):
                at = zl if way == 0 else 7 - zl
                d = 7 - (s - at) if way == 0 else s - at
                d = jnp.clip(d, 0, 7)

                if s:

                    @pl.when(jnp.logical_and(at <= s, at > 0))
                    def _():
                        line_copy(way, s - 1, e).wait_recv()
                        total = own1(d, e) + line_r[way, s - 1, e].astype(F32)
                        line_s[way, s, e] = total.astype(BF16)
                        line_copy(way, s, e).start()

                @pl.when(at == 0)
                def _():
                    line_s[way, s, e] = own1(d, e).astype(BF16)
                    line_copy(way, s, e).start()

        if s == 0:
            ring_steps((2, 7), (1, 5), (0, 3))
        if s == 1:
            ring_end(2, g_r2)
            ring_steps((1, 6), (0, 4))
        if s == 2:
            ring_steps((1, 7), (0, 5))
        if s == 3:
            ring_end(1, g_l2)
            ring_step(0, 6)
        if s == 4:
            for jj in range(4):
                cols = pl.ds(jj * SIZE, SIZE)
                in_grad[home_rows(h), cols] = dot(block(da1, h * 4 + jj), l1[jj], TN).astype(BF16)
                in_grad[home_rows(1 - h), cols] = dot(block(back, jj), l1[jj], TN).astype(BF16)
            ring_step(0, 7)
        if s == 6:
            ring_end(0, g_r1)

    for e in range(2):
        last[e] = own1(zl, e)
        for way in range(2):
            at = zl if way == 0 else 7 - zl

            @pl.when(at > 0)
            def _():
                line_copy(way, 6, e).wait_recv()
                last[e] += line_r[way, 6, e].astype(F32)

        for j in range(2):
            g_l1[:, 2 * e + j, :] = last[e, j] * scale

    for n in range(2):
        sent = xs.at[n, pl.ds(0, 63)]
        pltpu.make_async_copy(sent, sent, xs_sem.at[n]).wait()
    for n in range(5):
        sent = ps.at[n, pl.ds(0, PLANE - 1)]
        pltpu.make_async_copy(sent, sent, ps_sem.at[n]).wait()
    for c in range(8):
        back_copy(c).wait_send()
    for way in range(2):
        for k in range(24):
            gather_copy(way, k, other.at[way, k]).wait_send()
    for n in range(3):
        for s in range(8):
            ring_copy(n, 0, s).wait_send()
            if s < 7:
                ring_copy(n, 1, s).wait_send()
    for way in range(2):
        at = zl if way == 0 else 7 - zl
        for s in range(7):

            @pl.when(at <= s)
            def _():
                line_copy(way, s, 0).wait_send()
                line_copy(way, s, 1).wait_send()


def per_device(features_in, cotangent, left_one, right_one, left_two, right_two):
    vmem = pl.BlockSpec(memory_space=pltpu.VMEM)
    dma = pltpu.SemaphoreType.DMA
    square = (SIZE, SIZE)
    grad = jax.ShapeDtypeStruct((32, 4, SIZE), F32)
    arrived = pltpu.VMEM((8, 4, 2, 2, 16, TOK), BF16)
    eight = pltpu.VMEM((8,) + square, BF16)
    outs = pl.pallas_call(
        kernel,
        name="monarch",
        out_shape=(jax.ShapeDtypeStruct(features_in.shape, BF16), grad, grad, grad, grad),
        in_specs=[pl.BlockSpec(memory_space=pl.ANY)] * 6,
        out_specs=(vmem,) * 5,
        scratch_shapes=[
            pltpu.VMEM(features_in.shape, BF16),
            pltpu.VMEM(features_in.shape, BF16),
            pltpu.VMEM((4,) + square, BF16),
            pltpu.VMEM((4,) + square, BF16),
            pltpu.VMEM((4,) + square, BF16),
            pltpu.VMEM((4,) + square, BF16),
            dma((6,)),
            pltpu.VMEM(square, BF16),
            pltpu.VMEM(square, BF16),
            pltpu.VMEM(square, BF16),
            pltpu.VMEM((4,) + square, BF16),
            eight, eight, eight, eight, eight,
            pltpu.VMEM((2, 24, 64, SIZE), BF16),
            pltpu.VMEM((2, 64, 32, TOK), BF16),
            pltpu.VMEM((2, 64, 32, TOK), BF16),
            pltpu.VMEM((5, PLANE, 64, TOK), BF16),
            pltpu.VMEM((5, PLANE, 64, TOK), BF16),
            arrived, arrived, arrived, pltpu.VMEM((8, 4, 2, 2, 16, TOK), F32), arrived, arrived, arrived, arrived, arrived,
            pltpu.VMEM((4, 4, 2, 2, 16, TOK), BF16),
            pltpu.VMEM((3, 8) + square, F32),
            pltpu.VMEM((4,) + square, F32),
            pltpu.VMEM((2, 2, 32, SIZE), F32),
            pltpu.VMEM((3, 2, 8, 4, 32, SIZE), BF16),
            pltpu.VMEM((3, 2, 8, 4, 32, SIZE), BF16),
            pltpu.VMEM((2, 7, 2, 2, 32, SIZE), BF16),
            pltpu.VMEM((2, 7, 2, 2, 32, SIZE), BF16),
            dma((2,)), dma((2,)), dma((5,)), dma((5,)), dma((2, 8)),
            dma((2, 24)), dma((2, 24)), dma((3, 2, 8)), dma((3, 2, 8)), dma((2, 7, 2)), dma((2, 7, 2)),
        ],
        compiler_params=pltpu.CompilerParams(
            collective_id=0, has_side_effects=True, vmem_limit_bytes=56 << 20
        ),
        cost_estimate=pl.CostEstimate(
            flops=4_000_000_000, bytes_accessed=5_000_000, transcendentals=600_000
        ),
    )(features_in, cotangent, left_one, right_one, left_two, right_two)
    return outs


def solution(mesh):
    return jax.shard_map(
        per_device,
        mesh=mesh,
        in_specs=(
            P("dp", "block"),
            P("dp", "block"),
            P("block", None, None),
            P("block", None, None),
            P("block", None, None),
            P("block", None, None),
        ),
        out_specs=(
            P("dp", "block"),
            P("dp", "block", None),
            P("dp", "block", None),
            P("dp", "block", None),
            P("dp", "block", None),
        ),
        check_vma=False,
    )
```
